32 devices in a mesh: req: 16 (over z, x, core), mdl: 2 (over y).
Axes of the slice: x: 2, y: 2, z: 4, core: 2. Of those that a mesh axis runs over, the one named last changes fastest.
Arguments:
- hidden: bfloat16 [4096, 1536], P(('req', 'mdl')), may hold values from -6 to 6
- input_gain: float32 [1536], replicated, may hold values from 0.1 to 1.9
- gate_proj: bfloat16 [1536, 3072], P('req', 'mdl'), may hold values from -0.15625 to 0.15625
- value_proj: bfloat16 [1536, 3072], P('req', 'mdl'), may hold values from -0.15625 to 0.15625
- state_proj: bfloat16 [1536, 256], P('req'), may hold values from -0.15625 to 0.15625
- step_proj: bfloat16 [1536, 48], P('req', 'mdl'), may hold values from -0.15625 to 0.15625
- conv_value: float32 [5, 3072], P(None, 'mdl'), may hold values from -3 to 3
- conv_state: float32 [5, 256], replicated, may hold values from -3 to 3
- step_bias: float32 [48], P('mdl'), may hold values from -4 to -1
- decay_log: float32 [48], P('mdl'), may hold values from -4 to 0
- skip_gain: float32 [48], P('mdl'), may hold values from 0.5 to 1.5
- output_gain: float32 [3072], P('mdl'), may hold values from 0.1 to 1.9
- out_proj: bfloat16 [3072, 1536], P('mdl', 'req'), may hold values from -0.109375 to 0.109375
- state_start: float32 [32, 48, 64, 128], P('req', 'mdl'), may hold values from -0.8 to 0.8
- edge_value: bfloat16 [32, 3, 3072], P('req', None, 'mdl'), may hold values from -6 to 6
- edge_state: bfloat16 [32, 3, 256], P('req'), may hold values from -6 to 6
- lengths: int32 [32], P('req'), may hold values from 1 to 128, as said below
- accepted: int32 [32], P('req'), may hold values from 1 to 128, as said below
Outputs:
- mixed: bfloat16 [4096, 1536], P(('req', 'mdl'))
- state_final: float32 [32, 48, 64, 128], P(('req', 'mdl'))
- edge_final: bfloat16 [32, 3, 3328], P(('req', 'mdl'))
The draws below stay inside these ranges and needn't reach their ends.
Inputs may be any that keep to these rules, and one draw needn't show every extreme that they name: `lengths`: one request's draft fills all 128 slots. accepted[r] <= lengths[r]; the request whose draft fills all slots accepts all of it.
All inputs are finite; a program needn't handle non-finite values.
Results may differ from the reference program's by a relative error of at most 0.009.
Values may be sent and summed in bfloat16 or wider, within the bound.
A program may use at most 64 MiB of HBM per device.

```python
import jax
import jax.numpy as jnp
from jax import lax

D = 1536
H = 48
HEADDIM = 64
NS = 128
KC = 4
MAXLEN = 128
DI = 3072
REQS = 32
ROWS = 4096
N_MDL = 2


def shared_lengths(key):
    first = jax.random.fold_in(key, 101)
    second = jax.random.fold_in(key, 202)
    counts = jax.random.randint(first, (REQS,), 1, MAXLEN + 1)
    chosen = jax.random.randint(second, (), 0, REQS)
    full = jnp.arange(REQS) == chosen
    return (jnp.where(full, MAXLEN, counts).astype(jnp.int32), full)


def draw_lengths(key, part):
    return shared_lengths(key)[0]


def draw_accepted(key, part):
    counts, full = shared_lengths(key)
    raw = jax.random.randint(jax.random.fold_in(key, 303), (REQS,), 0, 1 << 20)
    taken = raw % counts + 1
    return jnp.where(full, MAXLEN, taken).astype(jnp.int32)


def block_scale(own_key, shape, pieces, smallest, top_value):
    def one(axis_at, parts):
        draws = jax.random.uniform(jax.random.fold_in(jax.random.fold_in(own_key, 6), axis_at), (parts,), jnp.float32, smallest / len(pieces), top_value / len(pieces))
        return jnp.repeat(jnp.exp(draws), shape[axis_at] // parts).reshape((-1,) + (1,) * (len(shape) - axis_at - 1))

    loudness = one(*pieces[0])
    for cut in pieces[1:]:
        loudness = loudness * one(*cut)
    return loudness


def bell_draw(rng, dims, scale, most, split=(), kind=jnp.bfloat16):
    array = scale * jax.random.normal(rng, dims, jnp.float32)
    if split:
        array = array * block_scale(rng, dims, split, -0.22, 0.18)
    return jnp.clip(array, -most, most).astype(kind)


def setup_inputs(seed: int = 0) -> dict:
    splits = jax.random.split(jax.random.key(seed), 19)
    hidden = bell_draw(splits[0], (ROWS, D), 1.0, 6.0, ((0, 32),))
    input_gain = jnp.clip(1.0 + 0.18 * jax.random.normal(splits[1], (D,), jnp.float32), 0.1, 1.9)
    gate_proj = bell_draw(splits[2], (D, DI), D ** -0.5, 0.15625, ((0, 16), (1, 2)))
    value_proj = bell_draw(splits[3], (D, DI), D ** -0.5, 0.15625, ((0, 16), (1, 2)))
    state_proj = bell_draw(splits[4], (D, 2 * NS), D ** -0.5, 0.15625, ((0, 16),))
    step_proj = bell_draw(splits[5], (D, H), D ** -0.5, 0.15625, ((0, 16), (1, 2)))
    conv_value = bell_draw(splits[6], (KC + 1, DI), 0.5, 3.0, ((1, 2),), jnp.float32)
    conv_state = bell_draw(splits[7], (KC + 1, 2 * NS), 0.5, 3.0, (), jnp.float32)
    step_bias = jnp.clip(-4.0 + 3.0 * jax.random.uniform(splits[8], (H,), jnp.float32) ** block_scale(splits[8], (H,), ((0, 2),), -0.2, 0.2), -4.0, -1.0)
    decay_log = jnp.clip(-4.0 + 4.0 * jax.random.uniform(splits[9], (H,), jnp.float32) ** block_scale(splits[9], (H,), ((0, 2),), -0.2, 0.2), -4.0, 0.0)
    skip_gain = jnp.clip(0.5 + 1.0 * jax.random.uniform(splits[10], (H,), jnp.float32) ** block_scale(splits[10], (H,), ((0, 2),), -0.2, 0.2), 0.5, 1.5)
    output_gain = jnp.clip(1.0 + 0.18 * jax.random.normal(splits[11], (DI,), jnp.float32), 0.1, 1.9)
    out_proj = bell_draw(splits[12], (DI, D), DI ** -0.5, 0.109375, ((0, 2), (1, 16)))
    state_start = bell_draw(splits[13], (REQS, H, HEADDIM, NS), 0.1, 0.8, ((0, 16), (1, 2)), jnp.float32)
    edge_value = bell_draw(splits[14], (REQS, KC - 1, DI), 1.0, 6.0, ((0, 16), (2, 2)))
    edge_state = bell_draw(splits[15], (REQS, KC - 1, 2 * NS), 1.0, 6.0, ((0, 16),))
    lengths = draw_lengths(jax.random.fold_in(splits[18], 71), 0)
    accepted = draw_accepted(jax.random.fold_in(splits[18], 71), 0)
    return {"hidden": hidden, "input_gain": input_gain, "gate_proj": gate_proj, "value_proj": value_proj, "state_proj": state_proj, "step_proj": step_proj, "conv_value": conv_value, "conv_state": conv_state, "step_bias": step_bias, "decay_log": decay_log, "skip_gain": skip_gain, "output_gain": output_gain, "out_proj": out_proj, "state_start": state_start, "edge_value": edge_value, "edge_state": edge_state, "lengths": lengths, "accepted": accepted}


EPSILON = 1e-05
HIGHEST = lax.Precision.HIGHEST

def request_scan(values, inputs_b, reads_c, steps, logs, start, last):
    positions = jnp.arange(values.shape[0], dtype=jnp.int32)

    def advance(carry, item):
        state, kept = carry
        value_t, input_t, read_t, step_t, log_t, where_t = item
        state = jnp.exp(log_t)[:, None, None] * state + (step_t[:, None] * value_t)[:, :, None] * input_t[None, None, :]
        output_t = jnp.einsum('hpn,n->hp', state, read_t, precision=HIGHEST)
        kept = jnp.where(where_t == last, state, kept)
        return ((state, kept), output_t)
    (state, kept), outputs = lax.scan(advance, (start, start), (values, inputs_b, reads_c, steps, logs, positions))
    return (outputs, kept)

def group_layer(weights, items):
    input_gain, gate_proj, value_proj, state_proj, step_proj, conv_value, conv_state, step_bias, decay_log, skip_gain, output_gain, out_proj = weights
    hidden, state_start, edge_value, edge_state, lengths, accepted = items
    requests, heads, head_dim, nstate = state_start.shape
    span = hidden.shape[0] // requests
    inner = heads * head_dim
    floats = hidden.astype(jnp.float32)
    normed = (floats * lax.rsqrt(lax.optimization_barrier(jnp.mean(floats * floats, -1, keepdims=True)) + EPSILON) * input_gain).astype(jnp.bfloat16)
    gates = jnp.dot(normed, gate_proj, preferred_element_type=jnp.float32).astype(jnp.bfloat16)
    values = jnp.dot(normed, value_proj, preferred_element_type=jnp.float32).astype(jnp.bfloat16)
    readers = jnp.dot(normed, state_proj, preferred_element_type=jnp.float32).astype(jnp.bfloat16)
    step_raw = jnp.dot(normed, step_proj, preferred_element_type=jnp.float32).astype(jnp.bfloat16)
    current = jnp.concatenate([values, readers], 1).reshape(requests, span, -1)
    edges = jnp.concatenate([edge_value, edge_state], 2)
    extended = jnp.concatenate([edges, current], 1).astype(jnp.float32)
    taps = jnp.concatenate([conv_value, conv_state], 1)
    width_k = taps.shape[0] - 1
    edge_count = width_k - 1
    convolved = taps[width_k][None, None, :] + jnp.zeros((requests, span, taps.shape[1]), jnp.float32)
    for shift in range(width_k):
        convolved = convolved + taps[shift][None, None, :] * extended[:, shift:shift + span]
    active = jax.nn.silu(convolved).astype(jnp.bfloat16).astype(jnp.float32)
    vals = active[..., :inner].reshape(requests, span, heads, head_dim)
    inputs_b = active[..., inner:inner + nstate]
    reads_c = active[..., inner + nstate:]
    steps = jax.nn.softplus(step_raw.astype(jnp.float32).reshape(requests, span, heads) + step_bias)
    logs = -steps * jnp.exp(decay_log)
    outputs, kept = jax.vmap(request_scan)(vals, inputs_b, reads_c, steps, logs, state_start, accepted - 1)
    outputs = outputs + skip_gain[:, None] * vals
    product = outputs.reshape(requests * span, inner) * jax.nn.silu(gates.astype(jnp.float32))
    scale = lax.rsqrt(lax.optimization_barrier(jnp.mean(product * product, -1)) + EPSILON)
    gated = (product * output_gain).astype(jnp.bfloat16)
    block = inner // N_MDL
    total = jnp.zeros((requests * span, out_proj.shape[1]), jnp.float32)
    for piece in range(N_MDL):
        term = jnp.dot(gated[:, piece * block:(piece + 1) * block], out_proj[piece * block:(piece + 1) * block], preferred_element_type=jnp.float32).astype(jnp.bfloat16)
        total = total + lax.optimization_barrier(term).astype(jnp.float32)
    live = (jnp.arange(span, dtype=jnp.int32)[None, :] < lengths[:, None]).reshape(-1).astype(jnp.float32)
    mixed = (total * scale[:, None] * live[:, None]).astype(jnp.bfloat16)
    picks = accepted[:, None] + jnp.arange(edge_count, dtype=jnp.int32)[None, :]
    edge_final = jnp.take_along_axis(extended, picks[:, :, None], axis=1).astype(jnp.bfloat16)
    return (mixed, kept, edge_final)

def reference(hidden, input_gain, gate_proj, value_proj, state_proj, step_proj, conv_value, conv_state, step_bias, decay_log, skip_gain, output_gain, out_proj, state_start, edge_value, edge_state, lengths, accepted):
    weights = (input_gain, gate_proj, value_proj, state_proj, step_proj, conv_value, conv_state, step_bias, decay_log, skip_gain, output_gain, out_proj)
    groups = state_start.shape[0] // N_MDL
    items = (hidden.reshape(groups, -1, hidden.shape[1]), state_start.reshape((groups, N_MDL) + state_start.shape[1:]), edge_value.reshape((groups, N_MDL) + edge_value.shape[1:]), edge_state.reshape((groups, N_MDL) + edge_state.shape[1:]), lengths.reshape(groups, N_MDL), accepted.reshape(groups, N_MDL))
    mixed, kept, edge_final = lax.map(lambda group: group_layer(weights, group), items)
    return (mixed.reshape(-1, mixed.shape[-1]), kept.reshape((-1,) + kept.shape[2:]), edge_final.reshape((-1,) + edge_final.shape[2:]))
```

```python
import jax
import jax.numpy as jnp
from jax import lax
from jax.sharding import PartitionSpec as P

EPSILON = 1e-05
HIGHEST = lax.Precision.HIGHEST


def local(
    hidden,
    input_gain,
    gate_proj,
    value_proj,
    state_proj,
    step_proj,
    conv_value,
    conv_state,
    step_bias,
    decay_log,
    skip_gain,
    output_gain,
    out_proj,
    state_start,
    edge_value,
    edge_state,
    lengths,
    accepted,
):
    requests, heads_here, head_dim, nstate = state_start.shape
    rows_dev = hidden.shape[0]
    span = rows_dev * lax.axis_size("mdl") // requests
    here_count = rows_dev // span
    group_rows = requests * span
    inner_here = heads_here * head_dim
    width_k = conv_value.shape[0] - 1
    edge_count = width_k - 1
    my_index = lax.axis_index("mdl")
    floats = hidden.astype(jnp.float32)
    normed = (
        floats * lax.rsqrt(jnp.mean(floats * floats, -1, keepdims=True) + EPSILON) * input_gain
    ).astype(jnp.bfloat16)
    widths = (gate_proj.shape[1], value_proj.shape[1], state_proj.shape[1], step_proj.shape[1])
    first_end = widths[0]
    second_end = first_end + widths[1]
    third_end = second_end + widths[2]
    whole = lax.all_gather(normed, "mdl", axis=0, tiled=True)
    packed = jnp.concatenate((gate_proj, value_proj, state_proj, step_proj), 1)
    joined_piece = lax.all_gather(packed, "req", axis=0, tiled=True)
    joined = jnp.dot(whole, joined_piece, preferred_element_type=jnp.float32)
    gates = joined[:, :first_end].astype(jnp.bfloat16)
    values = joined[:, first_end:second_end].astype(jnp.bfloat16)
    readers = joined[:, second_end:third_end].astype(jnp.bfloat16)
    step_raw = joined[:, third_end:].astype(jnp.bfloat16)
    current = jnp.concatenate([values, readers], 1).reshape(requests, span, -1)
    edges = jnp.concatenate([edge_value, edge_state], 2)
    extended = jnp.concatenate([edges, current], 1).astype(jnp.float32)
    taps = jnp.concatenate([conv_value, conv_state], 1)
    convolved = taps[width_k][None, None, :] + jnp.zeros(
        (requests, span, taps.shape[1]), jnp.float32
    )
    for shift in range(width_k):
        convolved = convolved + taps[shift][None, None, :] * extended[:, shift : shift + span]
    active = jax.nn.silu(convolved).astype(jnp.bfloat16)
    vals = active[..., :inner_here].reshape(requests, span, heads_here, head_dim)
    inputs_b = active[..., inner_here : inner_here + nstate]
    reads_c = active[..., inner_here + nstate :]
    vals_f = vals.astype(jnp.float32)
    steps = jax.nn.softplus(
        step_raw.astype(jnp.float32).reshape(requests, span, heads_here) + step_bias
    )
    logs = -steps * jnp.exp(decay_log)
    sooner = jnp.arange(span, dtype=jnp.int32)
    triangle = (sooner[:, None] >= sooner[None, :]).astype(jnp.float32)
    running = jnp.einsum("ts,gsh->gth", triangle, logs, precision=HIGHEST)
    intersection = jnp.einsum("gtn,gsn->gts", reads_c, inputs_b, preferred_element_type=jnp.float32)
    positions = jnp.arange(span, dtype=jnp.int32)
    lower = positions[:, None] >= positions[None, :]
    spread = jnp.where(
        lower[None, :, :, None], running[:, :, None, :] - running[:, None, :, :], -jnp.inf
    )
    kernel = intersection[..., None] * jnp.exp(spread) * steps[:, None, :, :]
    outputs = jnp.einsum("gtsh,gshp->gthp", kernel, vals_f, precision=HIGHEST)
    carried = jnp.einsum(
        "gtn,ghpn->gthp", reads_c.astype(jnp.float32), state_start, precision=HIGHEST
    )
    outputs = outputs + jnp.exp(running)[..., None] * carried + skip_gain[:, None] * vals_f
    product = outputs.reshape(group_rows, inner_here) * jax.nn.silu(gates.astype(jnp.float32))
    squares = jnp.sum(product * product, -1)
    gated = (product * output_gain).astype(jnp.bfloat16)
    total_squares = lax.psum(squares, "mdl")
    scale = lax.rsqrt(total_squares / (inner_here * lax.axis_size("mdl")) + EPSILON)
    partial_terms = jnp.dot(
        gated,
        lax.all_gather(out_proj, "req", axis=1, tiled=True),
        preferred_element_type=jnp.float32,
    )
    mine = lax.psum_scatter(
        partial_terms.astype(jnp.bfloat16), "mdl", scatter_dimension=0, tiled=True
    ).astype(jnp.float32)
    my_scale = lax.dynamic_slice_in_dim(scale, my_index * rows_dev, rows_dev, 0)
    my_lengths = lax.dynamic_slice_in_dim(lengths, my_index * here_count, here_count, 0)
    live = (positions[None, :] < my_lengths[:, None]).reshape(rows_dev).astype(jnp.float32)
    mixed = (mine * my_scale[:, None] * live[:, None]).astype(jnp.bfloat16)
    last = accepted - 1
    chosen = (positions[None, :] == last[:, None]).astype(jnp.float32)
    running_last = jnp.sum(chosen[:, :, None] * running, axis=1)
    before = positions[None, :] <= last[:, None]
    reach = jnp.where(before[:, :, None], running_last[:, None, :] - running, -jnp.inf)
    weights_s = jnp.exp(reach) * steps
    gathered_state = jnp.einsum(
        "gsh,gshp,gsn->ghpn", weights_s, vals_f, inputs_b.astype(jnp.float32), precision=HIGHEST
    )
    state_here = jnp.exp(running_last)[:, :, None, None] * state_start + gathered_state
    picks = accepted[:, None] + jnp.arange(edge_count, dtype=jnp.int32)[None, :]
    selected = jnp.take_along_axis(extended, picks[:, :, None], axis=1)
    value_edges = selected[..., :inner_here].reshape(requests, edge_count, heads_here, head_dim)
    value_edges = value_edges.transpose(0, 2, 1, 3).reshape(
        requests, heads_here, edge_count * head_dim
    )
    states_home, edges_home = (
        lax.all_to_all(
            state_here.reshape(requests, heads_here, head_dim * nstate).astype(jnp.bfloat16),
            "mdl",
            split_axis=0,
            concat_axis=1,
            tiled=True,
        ).astype(jnp.float32),
        lax.all_to_all(
            value_edges.astype(jnp.bfloat16), "mdl", split_axis=0, concat_axis=1, tiled=True
        ).astype(value_edges.dtype),
    )
    heads_all = states_home.shape[1]
    state_final = states_home.reshape(here_count, heads_all, head_dim, nstate)
    edges_home = edges_home.reshape(here_count, heads_all, edge_count, head_dim).transpose(
        0, 2, 1, 3
    )
    edges_home = edges_home.reshape(here_count, edge_count, heads_all * head_dim)
    state_edges = lax.dynamic_slice_in_dim(
        selected[..., inner_here:], my_index * here_count, here_count, 0
    )
    edge_final = jnp.concatenate([edges_home, state_edges], 2).astype(jnp.bfloat16)
    return (mixed, state_final, edge_final)


def solution(mesh):
    return jax.shard_map(
        local,
        mesh=mesh,
        in_specs=(
            P(("req", "mdl"), None),
            P(),
            P("req", "mdl"),
            P("req", "mdl"),
            P("req", None),
            P("req", "mdl"),
            P(None, "mdl"),
            P(),
            P("mdl"),
            P("mdl"),
            P("mdl"),
            P("mdl"),
            P("mdl", "req"),
            P("req", "mdl", None, None),
            P("req", None, "mdl"),
            P("req", None, None),
            P("req"),
            P("req"),
        ),
        out_specs=(
            P(("req", "mdl"), None),
            P(("req", "mdl"), None, None, None),
            P(("req", "mdl"), None, None),
        ),
        check_vma=False,
    )
```

```python
import jax
import jax.numpy as jnp
from jax import lax
from jax.experimental import pallas as pl
from jax.experimental.pallas import tpu as pltpu
from jax.sharding import PartitionSpec as P

EPSILON = 1e-05
HIGHEST = lax.Precision.HIGHEST
MESH = pl.DeviceIdType.MESH
CHUNK = 16


def ring_fits(rows):
    return (
        lax.axis_size("mdl") == 2
        and lax.axis_size("req") % 4 == 0
        and lax.axis_size("req") >= 8
        and rows % (2 * CHUNK) == 0
    )


def ring_kernel(
    count,
    own_ref,
    turned_ref,
    normed_ref,
    packed_ref,
    out_ref,
    whole_ref,
    send_sem,
    recv_sem,
    twin_send,
    twin_recv,
    pair_sem,
    local_sem,
):
    chips = count // 2
    depth = chips // 2
    me = lax.axis_index("req")
    side = lax.axis_index("mdl")
    core = me % 2
    chip = me // 2
    x = chip % 2
    z = chip // 2
    place = z + x * (chips - 1 - 2 * z)

    def at(spot, which):
        spot = (spot + 2 * chips) % chips
        far = spot // depth
        level = spot + far * (chips - 1 - 2 * spot)
        return (level * 2 + far) * 2 + which

    right, left, twin = at(place + 1, core), at(place - 1, core), at(place, 1 - core)
    partner = 1 - side
    barrier = pltpu.get_barrier_semaphore()
    for other in (right, left, twin):
        pl.semaphore_signal(barrier, inc=1, device_id=(other, side), device_id_type=MESH)
    pl.semaphore_signal(barrier, inc=1, device_id=(me, partner), device_id_type=MESH)
    pl.semaphore_wait(barrier, 4)

    half = own_ref.shape[0] // 2
    pieces = [("p", k * CHUNK, CHUNK) for k in range(half // CHUNK)] + [("o", 0, half)]

    def views(owner, way, piece, first):
        kind, start, size = piece
        rows = pl.ds(way * half + start, size)
        target = (packed_ref if kind == "p" else out_ref).at[owner, rows]
        if first:
            return (own_ref if kind == "p" else turned_ref).at[rows], target
        return target, target

    def hop(way, step, k):
        owner = at(place - step if way == 0 else place + step, core)
        source, target = views(owner, way, pieces[k], step == 0)
        return pltpu.make_async_remote_copy(
            src_ref=source,
            dst_ref=target,
            send_sem=send_sem.at[way, step, k],
            recv_sem=recv_sem.at[way, step, k],
            device_id=(right if way == 0 else left, side),
            device_id_type=MESH,
        )

    def across(way, step, k):
        owner = at(place - step if way == 0 else place + step, core)
        source, target = views(owner, way, pieces[k], step == 0)
        return pltpu.make_async_remote_copy(
            src_ref=source,
            dst_ref=target,
            send_sem=twin_send.at[way, step, k],
            recv_sem=twin_recv.at[way, step, k],
            device_id=(twin, side),
            device_id_type=MESH,
        )

    started = []
    for k in range(len(pieces)):
        for way in range(2):
            copy = hop(way, 0, k)
            copy.start()
            started.append(copy)
    rows_copy = pltpu.make_async_remote_copy(
        src_ref=normed_ref,
        dst_ref=whole_ref.at[side],
        send_sem=pair_sem.at[0],
        recv_sem=pair_sem.at[1],
        device_id=(me, partner),
        device_id_type=MESH,
    )
    rows_copy.start()
    locals_ = [
        pltpu.make_async_copy(own_ref, packed_ref.at[me], local_sem.at[0]),
        pltpu.make_async_copy(turned_ref, out_ref.at[me], local_sem.at[1]),
        pltpu.make_async_copy(normed_ref, whole_ref.at[side], local_sem.at[2]),
    ]
    for copy in locals_:
        copy.start()
    crossed = []
    for step in range(chips):
        for k in range(len(pieces)):
            for way in range(2):
                if step > 0:
                    hop(way, step - 1, k).wait_recv()
                    if step < chips - 1:
                        copy = hop(way, step, k)
                        copy.start()
                        started.append(copy)
                copy = across(way, step, k)
                copy.start()
                crossed.append(copy)
    for copy in locals_:
        copy.wait()
    for copy in started:
        copy.wait_send()
    for copy in crossed:
        copy.wait()
    rows_copy.wait()


def ring_gather(packed, turned, normed):
    count = lax.axis_size("req")
    chips = count // 2
    parts = packed.shape[0] // (2 * CHUNK) + 1
    anywhere = pl.BlockSpec(memory_space=pl.ANY)
    gathered, columns, whole = pl.pallas_call(
        lambda *refs: ring_kernel(count, *refs),
        out_shape=(
            jax.ShapeDtypeStruct((count,) + packed.shape, packed.dtype),
            jax.ShapeDtypeStruct((count,) + turned.shape, turned.dtype),
            jax.ShapeDtypeStruct((2,) + normed.shape, normed.dtype),
        ),
        in_specs=[anywhere] * 3,
        out_specs=(anywhere,) * 3,
        scratch_shapes=[
            pltpu.SemaphoreType.DMA((2, chips - 1, parts)),
            pltpu.SemaphoreType.DMA((2, chips - 1, parts)),
            pltpu.SemaphoreType.DMA((2, chips, parts)),
            pltpu.SemaphoreType.DMA((2, chips, parts)),
            pltpu.SemaphoreType.DMA((2,)),
            pltpu.SemaphoreType.DMA((3,)),
        ],
        compiler_params=pltpu.CompilerParams(collective_id=0, has_side_effects=True),
    )(packed, turned, normed)
    return (
        gathered.reshape(-1, packed.shape[1]),
        columns.reshape(-1, turned.shape[1]),
        whole.reshape(-1, normed.shape[1]),
    )


def gather_all(packed, out_proj, normed):
    if ring_fits(packed.shape[0]):
        spare = -packed.shape[1] % 128
        packed = jnp.pad(packed, ((0, 0), (0, spare)))
        return ring_gather(packed, out_proj.T, normed)
    return (
        lax.all_gather(packed, "req", axis=0, tiled=True),
        lax.all_gather(out_proj.T, "req", axis=0, tiled=True),
        lax.all_gather(normed, "mdl", axis=0, tiled=True),
    )


def swap(array):
    return lax.ppermute(array, "mdl", [(0, 1), (1, 0)])


def local(
    hidden,
    input_gain,
    gate_proj,
    value_proj,
    state_proj,
    step_proj,
    conv_value,
    conv_state,
    step_bias,
    decay_log,
    skip_gain,
    output_gain,
    out_proj,
    state_start,
    edge_value,
    edge_state,
    lengths,
    accepted,
):
    requests, heads_here, head_dim, nstate = state_start.shape
    rows_dev = hidden.shape[0]
    span = rows_dev * lax.axis_size("mdl") // requests
    here_count = rows_dev // span
    group_rows = requests * span
    inner_here = heads_here * head_dim
    width_k = conv_value.shape[0] - 1
    edge_count = width_k - 1
    my_index = lax.axis_index("mdl")
    floats = hidden.astype(jnp.float32)
    normed = (
        floats * lax.rsqrt(jnp.mean(floats * floats, -1, keepdims=True) + EPSILON) * input_gain
    ).astype(jnp.bfloat16)
    widths = (gate_proj.shape[1], value_proj.shape[1], state_proj.shape[1], step_proj.shape[1])
    first_end = widths[0]
    second_end = first_end + widths[1]
    third_end = second_end + widths[2]
    fourth_end = third_end + widths[3]
    packed = jnp.concatenate((gate_proj, value_proj, state_proj, step_proj), 1)
    joined_piece, out_turned, whole = gather_all(packed, out_proj, normed)
    joined = jnp.dot(whole, joined_piece, preferred_element_type=jnp.float32)
    gates = joined[:, :first_end].astype(jnp.bfloat16)
    values = joined[:, first_end:second_end].astype(jnp.bfloat16)
    readers = joined[:, second_end:third_end].astype(jnp.bfloat16)
    step_raw = joined[:, third_end:fourth_end].astype(jnp.bfloat16)
    current = jnp.concatenate([values, readers], 1).reshape(requests, span, -1)
    edges = jnp.concatenate([edge_value, edge_state], 2)
    extended = jnp.concatenate([edges, current], 1).astype(jnp.float32)
    taps = jnp.concatenate([conv_value, conv_state], 1)
    convolved = taps[width_k][None, None, :] + jnp.zeros(
        (requests, span, taps.shape[1]), jnp.float32
    )
    for shift in range(width_k):
        convolved = convolved + taps[shift][None, None, :] * extended[:, shift : shift + span]
    active = jax.nn.silu(convolved).astype(jnp.bfloat16)
    vals = active[..., :inner_here].reshape(requests, span, heads_here, head_dim)
    inputs_b = active[..., inner_here : inner_here + nstate]
    reads_c = active[..., inner_here + nstate :]
    vals_f = vals.astype(jnp.float32)
    steps = jax.nn.softplus(
        step_raw.astype(jnp.float32).reshape(requests, span, heads_here) + step_bias
    )
    logs = -steps * jnp.exp(decay_log)
    sooner = jnp.arange(span, dtype=jnp.int32)
    triangle = (sooner[:, None] >= sooner[None, :]).astype(jnp.float32)
    running = jnp.einsum("ts,gsh->gth", triangle, logs, precision=HIGHEST)
    intersection = jnp.einsum("gtn,gsn->gts", reads_c, inputs_b, preferred_element_type=jnp.float32)
    positions = jnp.arange(span, dtype=jnp.int32)
    lower = positions[:, None] >= positions[None, :]
    spread = jnp.where(
        lower[None, :, :, None], running[:, :, None, :] - running[:, None, :, :], -jnp.inf
    )
    kernel = intersection[..., None] * jnp.exp(spread) * steps[:, None, :, :]
    outputs = jnp.einsum("gtsh,gshp->gthp", kernel, vals_f, precision=HIGHEST)
    carried = jnp.einsum(
        "gtn,ghpn->gthp", reads_c.astype(jnp.float32), state_start, precision=HIGHEST
    )
    outputs = outputs + jnp.exp(running)[..., None] * carried + skip_gain[:, None] * vals_f
    product = outputs.reshape(group_rows, inner_here) * jax.nn.silu(gates.astype(jnp.float32))
    squares = jnp.sum(product * product, -1)
    gated = (product * output_gain).astype(jnp.bfloat16)
    paired = lax.axis_size("mdl") == 2
    total_squares = squares + swap(squares) if paired else lax.psum(squares, "mdl")
    scale = lax.rsqrt(total_squares / (inner_here * lax.axis_size("mdl")) + EPSILON)
    partial_terms = lax.dot_general(
        gated, out_turned, (((1,), (1,)), ((), ())), preferred_element_type=jnp.float32
    ).astype(jnp.bfloat16)
    if paired:
        theirs = lax.dynamic_slice_in_dim(
            partial_terms, (1 - my_index) * rows_dev, rows_dev, 0
        )
        mine = lax.dynamic_slice_in_dim(partial_terms, my_index * rows_dev, rows_dev, 0)
        mine = mine.astype(jnp.float32) + swap(theirs).astype(jnp.float32)
    else:
        mine = lax.psum_scatter(
            partial_terms, "mdl", scatter_dimension=0, tiled=True
        ).astype(jnp.float32)
    my_scale = lax.dynamic_slice_in_dim(scale, my_index * rows_dev, rows_dev, 0)
    my_lengths = lax.dynamic_slice_in_dim(lengths, my_index * here_count, here_count, 0)
    live = (positions[None, :] < my_lengths[:, None]).reshape(rows_dev).astype(jnp.float32)
    mixed = (mine * my_scale[:, None] * live[:, None]).astype(jnp.bfloat16)
    last = accepted - 1
    chosen = (positions[None, :] == last[:, None]).astype(jnp.float32)
    running_last = jnp.sum(chosen[:, :, None] * running, axis=1)
    before = positions[None, :] <= last[:, None]
    reach = jnp.where(before[:, :, None], running_last[:, None, :] - running, -jnp.inf)
    weights_s = jnp.exp(reach) * steps
    gathered_state = jnp.einsum(
        "gsh,gshp,gsn->ghpn", weights_s, vals_f, inputs_b.astype(jnp.float32), precision=HIGHEST
    )
    state_here = jnp.exp(running_last)[:, :, None, None] * state_start + gathered_state
    picks = accepted[:, None] + jnp.arange(edge_count, dtype=jnp.int32)[None, :]
    selected = jnp.take_along_axis(extended, picks[:, :, None], axis=1)
    if paired:
        def to_owner(array, kind):
            sent = lax.dynamic_slice_in_dim(array, (1 - my_index) * here_count, here_count, 0)
            kept = lax.dynamic_slice_in_dim(array, my_index * here_count, here_count, 0)
            come = swap(sent.astype(jnp.bfloat16)).astype(kind)
            kept = kept.astype(kind)
            first = my_index == 0
            return jnp.where(first, kept, come), jnp.where(first, come, kept)

        state_final = jnp.concatenate(to_owner(state_here, jnp.float32), 1)
        edges_home = jnp.concatenate(to_owner(selected[..., :inner_here], selected.dtype), 2)
    else:
        value_edges = selected[..., :inner_here].reshape(requests, edge_count, heads_here, head_dim)
        value_edges = value_edges.transpose(0, 2, 1, 3).reshape(
            requests, heads_here, edge_count * head_dim
        )
        states_home, edges_home = (
            lax.all_to_all(
                state_here.reshape(requests, heads_here, head_dim * nstate).astype(jnp.bfloat16),
                "mdl",
                split_axis=0,
                concat_axis=1,
                tiled=True,
            ).astype(jnp.float32),
            lax.all_to_all(
                value_edges.astype(jnp.bfloat16), "mdl", split_axis=0, concat_axis=1, tiled=True
            ).astype(value_edges.dtype),
        )
        heads_all = states_home.shape[1]
        state_final = states_home.reshape(here_count, heads_all, head_dim, nstate)
        edges_home = edges_home.reshape(here_count, heads_all, edge_count, head_dim).transpose(
            0, 2, 1, 3
        )
        edges_home = edges_home.reshape(here_count, edge_count, heads_all * head_dim)
    state_edges = lax.dynamic_slice_in_dim(
        selected[..., inner_here:], my_index * here_count, here_count, 0
    )
    edge_final = jnp.concatenate([edges_home, state_edges], 2).astype(jnp.bfloat16)
    return (mixed, state_final, edge_final)


def solution(mesh):
    return jax.shard_map(
        local,
        mesh=mesh,
        in_specs=(
            P(("req", "mdl"), None),
            P(),
            P("req", "mdl"),
            P("req", "mdl"),
            P("req", None),
            P("req", "mdl"),
            P(None, "mdl"),
            P(),
            P("mdl"),
            P("mdl"),
            P("mdl"),
            P("mdl"),
            P("mdl", "req"),
            P("req", "mdl", None, None),
            P("req", None, "mdl"),
            P("req", None, None),
            P("req"),
            P("req"),
        ),
        out_specs=(
            P(("req", "mdl"), None),
            P(("req", "mdl"), None, None, None),
            P(("req", "mdl"), None, None),
        ),
        check_vma=False,
    )
```

```python
import jax
import jax.numpy as jnp
from jax import lax
from jax.experimental import pallas as pl
from jax.experimental.pallas import tpu as pltpu
from jax.sharding import PartitionSpec as P

EPSILON = 1e-05
HIGHEST = lax.Precision.HIGHEST
MESH = pl.DeviceIdType.MESH
CHUNK = 16


def ring_fits(rows):
    return (
        lax.axis_size("mdl") == 2
        and lax.axis_size("req") % 4 == 0
        and lax.axis_size("req") >= 8
        and rows % (2 * CHUNK) == 0
    )


def ring_kernel(
    count,
    own_ref,
    normed_ref,
    packed_ref,
    whole_ref,
    send_sem,
    recv_sem,
    twin_send,
    twin_recv,
    pair_sem,
    local_sem,
):
    chips = count // 2
    depth = chips // 2
    me = lax.axis_index("req")
    side = lax.axis_index("mdl")
    core = me % 2
    chip = me // 2
    x = chip % 2
    z = chip // 2
    place = z + x * (chips - 1 - 2 * z)

    def at(spot, which):
        spot = (spot + 2 * chips) % chips
        far = spot // depth
        level = spot + far * (chips - 1 - 2 * spot)
        return (level * 2 + far) * 2 + which

    right, left, twin = at(place + 1, core), at(place - 1, core), at(place, 1 - core)
    partner = 1 - side
    barrier = pltpu.get_barrier_semaphore()
    for other in (right, left, twin):
        pl.semaphore_signal(barrier, inc=1, device_id=(other, side), device_id_type=MESH)
    pl.semaphore_signal(barrier, inc=1, device_id=(me, partner), device_id_type=MESH)
    pl.semaphore_wait(barrier, 4)

    half = own_ref.shape[0] // 2
    pieces = [k * CHUNK for k in range(half // CHUNK)]

    def views(owner, way, piece, first):
        rows = pl.ds(way * half + piece, CHUNK)
        target = packed_ref.at[owner, rows]
        return (own_ref.at[rows] if first else target), target

    def hop(way, step, k):
        owner = at(place - step if way == 0 else place + step, core)
        source, target = views(owner, way, pieces[k], step == 0)
        return pltpu.make_async_remote_copy(
            src_ref=source,
            dst_ref=target,
            send_sem=send_sem.at[way, step, k],
            recv_sem=recv_sem.at[way, step, k],
            device_id=(right if way == 0 else left, side),
            device_id_type=MESH,
        )

    def across(way, step, k):
        owner = at(place - step if way == 0 else place + step, core)
        source, target = views(owner, way, pieces[k], step == 0)
        return pltpu.make_async_remote_copy(
            src_ref=source,
            dst_ref=target,
            send_sem=twin_send.at[way, step, k],
            recv_sem=twin_recv.at[way, step, k],
            device_id=(twin, side),
            device_id_type=MESH,
        )

    started = []
    for k in range(len(pieces)):
        for way in range(2):
            copy = hop(way, 0, k)
            copy.start()
            started.append(copy)
    rows_copy = pltpu.make_async_remote_copy(
        src_ref=normed_ref,
        dst_ref=whole_ref.at[side],
        send_sem=pair_sem.at[0],
        recv_sem=pair_sem.at[1],
        device_id=(me, partner),
        device_id_type=MESH,
    )
    rows_copy.start()
    locals_ = [
        pltpu.make_async_copy(own_ref, packed_ref.at[me], local_sem.at[0]),
        pltpu.make_async_copy(normed_ref, whole_ref.at[side], local_sem.at[1]),
    ]
    for copy in locals_:
        copy.start()
    crossed = []
    for step in range(chips):
        for k in range(len(pieces)):
            for way in range(2):
                if step > 0:
                    hop(way, step - 1, k).wait_recv()
                    if step < chips - 1:
                        copy = hop(way, step, k)
                        copy.start()
                        started.append(copy)
                copy = across(way, step, k)
                copy.start()
                crossed.append(copy)
    for copy in locals_:
        copy.wait()
    for copy in started:
        copy.wait_send()
    for copy in crossed:
        copy.wait()
    rows_copy.wait()


def ring_gather(packed, normed):
    count = lax.axis_size("req")
    chips = count // 2
    parts = packed.shape[0] // (2 * CHUNK)
    anywhere = pl.BlockSpec(memory_space=pl.ANY)
    gathered, whole = pl.pallas_call(
        lambda *refs: ring_kernel(count, *refs),
        out_shape=(
            jax.ShapeDtypeStruct((count,) + packed.shape, packed.dtype),
            jax.ShapeDtypeStruct((2,) + normed.shape, normed.dtype),
        ),
        in_specs=[anywhere] * 2,
        out_specs=(anywhere,) * 2,
        scratch_shapes=[
            pltpu.SemaphoreType.DMA((2, chips - 1, parts)),
            pltpu.SemaphoreType.DMA((2, chips - 1, parts)),
            pltpu.SemaphoreType.DMA((2, chips, parts)),
            pltpu.SemaphoreType.DMA((2, chips, parts)),
            pltpu.SemaphoreType.DMA((2,)),
            pltpu.SemaphoreType.DMA((2,)),
        ],
        compiler_params=pltpu.CompilerParams(collective_id=0, has_side_effects=True),
    )(packed, normed)
    return (
        gathered.reshape(-1, packed.shape[1]),
        whole.reshape(-1, normed.shape[1]),
    )


def gather_all(packed, normed):
    if ring_fits(packed.shape[0]):
        spare = -packed.shape[1] % 128
        packed = jnp.pad(packed, ((0, 0), (0, spare)))
        return ring_gather(packed, normed)
    return (
        lax.all_gather(packed, "req", axis=0, tiled=True),
        lax.all_gather(normed, "mdl", axis=0, tiled=True),
    )


def swap(array):
    return lax.ppermute(array, "mdl", [(0, 1), (1, 0)])


def local(
    hidden,
    input_gain,
    gate_proj,
    value_proj,
    state_proj,
    step_proj,
    conv_value,
    conv_state,
    step_bias,
    decay_log,
    skip_gain,
    output_gain,
    out_proj,
    state_start,
    edge_value,
    edge_state,
    lengths,
    accepted,
):
    requests, heads_here, head_dim, nstate = state_start.shape
    rows_dev = hidden.shape[0]
    span = rows_dev * lax.axis_size("mdl") // requests
    here_count = rows_dev // span
    group_rows = requests * span
    inner_here = heads_here * head_dim
    width_k = conv_value.shape[0] - 1
    edge_count = width_k - 1
    my_index = lax.axis_index("mdl")
    floats = hidden.astype(jnp.float32)
    normed = (
        floats * lax.rsqrt(jnp.mean(floats * floats, -1, keepdims=True) + EPSILON) * input_gain
    ).astype(jnp.bfloat16)
    widths = (gate_proj.shape[1], value_proj.shape[1], state_proj.shape[1], step_proj.shape[1])
    first_end = widths[0]
    second_end = first_end + widths[1]
    third_end = second_end + widths[2]
    fourth_end = third_end + widths[3]
    packed = jnp.concatenate((gate_proj, value_proj, state_proj, step_proj), 1)
    out_turned = lax.all_gather(out_proj.T, "req", axis=0, tiled=True)
    joined_piece, whole = gather_all(packed, normed)
    joined = jnp.dot(whole, joined_piece, preferred_element_type=jnp.float32)
    gates = joined[:, :first_end].astype(jnp.bfloat16)
    values = joined[:, first_end:second_end].astype(jnp.bfloat16)
    readers = joined[:, second_end:third_end].astype(jnp.bfloat16)
    step_raw = joined[:, third_end:fourth_end].astype(jnp.bfloat16)
    current = jnp.concatenate([values, readers], 1).reshape(requests, span, -1)
    edges = jnp.concatenate([edge_value, edge_state], 2)
    extended = jnp.concatenate([edges, current], 1).astype(jnp.float32)
    taps = jnp.concatenate([conv_value, conv_state], 1)
    convolved = taps[width_k][None, None, :] + jnp.zeros(
        (requests, span, taps.shape[1]), jnp.float32
    )
    for shift in range(width_k):
        convolved = convolved + taps[shift][None, None, :] * extended[:, shift : shift + span]
    active = jax.nn.silu(convolved).astype(jnp.bfloat16)
    vals = active[..., :inner_here].reshape(requests, span, heads_here, head_dim)
    inputs_b = active[..., inner_here : inner_here + nstate]
    reads_c = active[..., inner_here + nstate :]
    vals_f = vals.astype(jnp.float32)
    steps = jax.nn.softplus(
        step_raw.astype(jnp.float32).reshape(requests, span, heads_here) + step_bias
    )
    logs = -steps * jnp.exp(decay_log)
    sooner = jnp.arange(span, dtype=jnp.int32)
    triangle = (sooner[:, None] >= sooner[None, :]).astype(jnp.float32)
    running = jnp.einsum("ts,gsh->gth", triangle, logs, precision=HIGHEST)
    intersection = jnp.einsum("gtn,gsn->gts", reads_c, inputs_b, preferred_element_type=jnp.float32)
    positions = jnp.arange(span, dtype=jnp.int32)
    lower = positions[:, None] >= positions[None, :]
    spread = jnp.where(
        lower[None, :, :, None], running[:, :, None, :] - running[:, None, :, :], -jnp.inf
    )
    kernel = intersection[..., None] * jnp.exp(spread) * steps[:, None, :, :]
    outputs = jnp.einsum(
        "gtsh,gshp->gthp", kernel.astype(jnp.bfloat16), vals, preferred_element_type=jnp.float32
    )
    carried = jnp.einsum(
        "gtn,ghpn->gthp",
        reads_c,
        state_start.astype(jnp.bfloat16),
        preferred_element_type=jnp.float32,
    )
    outputs = outputs + jnp.exp(running)[..., None] * carried + skip_gain[:, None] * vals_f
    product = outputs.reshape(group_rows, inner_here) * jax.nn.silu(gates.astype(jnp.float32))
    squares = jnp.sum(product * product, -1)
    gated = (product * output_gain).astype(jnp.bfloat16)
    paired = lax.axis_size("mdl") == 2
    total_squares = squares + swap(squares) if paired else lax.psum(squares, "mdl")
    scale = lax.rsqrt(total_squares / (inner_here * lax.axis_size("mdl")) + EPSILON)
    partial_terms = lax.dot_general(
        gated, out_turned, (((1,), (1,)), ((), ())), preferred_element_type=jnp.float32
    ).astype(jnp.bfloat16)
    if paired:
        theirs = lax.dynamic_slice_in_dim(
            partial_terms, (1 - my_index) * rows_dev, rows_dev, 0
        )
        mine = lax.dynamic_slice_in_dim(partial_terms, my_index * rows_dev, rows_dev, 0)
        mine = mine.astype(jnp.float32) + swap(theirs).astype(jnp.float32)
    else:
        mine = lax.psum_scatter(
            partial_terms, "mdl", scatter_dimension=0, tiled=True
        ).astype(jnp.float32)
    my_scale = lax.dynamic_slice_in_dim(scale, my_index * rows_dev, rows_dev, 0)
    my_lengths = lax.dynamic_slice_in_dim(lengths, my_index * here_count, here_count, 0)
    live = (positions[None, :] < my_lengths[:, None]).reshape(rows_dev).astype(jnp.float32)
    mixed = (mine * my_scale[:, None] * live[:, None]).astype(jnp.bfloat16)
    last = accepted - 1
    chosen = (positions[None, :] == last[:, None]).astype(jnp.float32)
    running_last = jnp.sum(chosen[:, :, None] * running, axis=1)
    before = positions[None, :] <= last[:, None]
    reach = jnp.where(before[:, :, None], running_last[:, None, :] - running, -jnp.inf)
    weights_s = jnp.exp(reach) * steps
    gathered_state = jnp.einsum(
        "gshp,gsn->ghpn",
        (weights_s[..., None] * vals_f).astype(jnp.bfloat16),
        inputs_b,
        preferred_element_type=jnp.float32,
    )
    state_here = jnp.exp(running_last)[:, :, None, None] * state_start + gathered_state
    picks = accepted[:, None] + jnp.arange(edge_count, dtype=jnp.int32)[None, :]
    selected = jnp.take_along_axis(extended, picks[:, :, None], axis=1)
    if paired:
        def to_owner(array, kind):
            sent = lax.dynamic_slice_in_dim(array, (1 - my_index) * here_count, here_count, 0)
            kept = lax.dynamic_slice_in_dim(array, my_index * here_count, here_count, 0)
            come = swap(sent.astype(jnp.bfloat16)).astype(kind)
            kept = kept.astype(kind)
            first = my_index == 0
            return jnp.where(first, kept, come), jnp.where(first, come, kept)

        state_final = jnp.concatenate(to_owner(state_here, jnp.float32), 1)
        edges_home = jnp.concatenate(to_owner(selected[..., :inner_here], selected.dtype), 2)
    else:
        value_edges = selected[..., :inner_here].reshape(requests, edge_count, heads_here, head_dim)
        value_edges = value_edges.transpose(0, 2, 1, 3).reshape(
            requests, heads_here, edge_count * head_dim
        )
        states_home, edges_home = (
            lax.all_to_all(
                state_here.reshape(requests, heads_here, head_dim * nstate).astype(jnp.bfloat16),
                "mdl",
                split_axis=0,
                concat_axis=1,
                tiled=True,
            ).astype(jnp.float32),
            lax.all_to_all(
                value_edges.astype(jnp.bfloat16), "mdl", split_axis=0, concat_axis=1, tiled=True
            ).astype(value_edges.dtype),
        )
        heads_all = states_home.shape[1]
        state_final = states_home.reshape(here_count, heads_all, head_dim, nstate)
        edges_home = edges_home.reshape(here_count, heads_all, edge_count, head_dim).transpose(
            0, 2, 1, 3
        )
        edges_home = edges_home.reshape(here_count, edge_count, heads_all * head_dim)
    state_edges = lax.dynamic_slice_in_dim(
        selected[..., inner_here:], my_index * here_count, here_count, 0
    )
    edge_final = jnp.concatenate([edges_home, state_edges], 2).astype(jnp.bfloat16)
    return (mixed, state_final, edge_final)


def solution(mesh):
    return jax.shard_map(
        local,
        mesh=mesh,
        in_specs=(
            P(("req", "mdl"), None),
            P(),
            P("req", "mdl"),
            P("req", "mdl"),
            P("req", None),
            P("req", "mdl"),
            P(None, "mdl"),
            P(),
            P("mdl"),
            P("mdl"),
            P("mdl"),
            P("mdl"),
            P("mdl", "req"),
            P("req", "mdl", None, None),
            P("req", None, "mdl"),
            P("req", None, None),
            P("req"),
            P("req"),
        ),
        out_specs=(
            P(("req", "mdl"), None),
            P(("req", "mdl"), None, None, None),
            P(("req", "mdl"), None, None),
        ),
        check_vma=False,
    )
```

```python
import jax
import jax.numpy as jnp
from jax import lax
from jax.experimental import pallas as pl
from jax.experimental.pallas import tpu as pltpu
from jax.sharding import PartitionSpec as P

EPSILON = 1e-05
HIGHEST = lax.Precision.HIGHEST
MESH = pl.DeviceIdType.MESH
CHUNK = 16


def ring_fits(rows):
    return (
        lax.axis_size("mdl") == 2
        and lax.axis_size("req") % 4 == 0
        and lax.axis_size("req") >= 8
        and rows % (2 * CHUNK) == 0
    )


def ring_kernel(
    count,
    own_ref,
    turned_ref,
    normed_ref,
    packed_ref,
    out_ref,
    whole_ref,
    send_sem,
    recv_sem,
    twin_send,
    twin_recv,
    pair_sem,
    local_sem,
):
    chips = count // 2
    depth = chips // 2
    me = lax.axis_index("req")
    side = lax.axis_index("mdl")
    core = me % 2
    chip = me // 2
    x = chip % 2
    z = chip // 2
    place = z + x * (chips - 1 - 2 * z)

    def at(spot, which):
        spot = (spot + 2 * chips) % chips
        far = spot // depth
        level = spot + far * (chips - 1 - 2 * spot)
        return (level * 2 + far) * 2 + which

    right, left, twin = at(place + 1, core), at(place - 1, core), at(place, 1 - core)
    partner = 1 - side
    barrier = pltpu.get_barrier_semaphore()
    for other in (right, left, twin):
        pl.semaphore_signal(barrier, inc=1, device_id=(other, side), device_id_type=MESH)
    pl.semaphore_signal(barrier, inc=1, device_id=(me, partner), device_id_type=MESH)
    pl.semaphore_wait(barrier, 4)

    half = own_ref.shape[0] // 2
    pieces = [("p", k * CHUNK, CHUNK) for k in range(half // CHUNK)] + [("o", 0, half)]

    def views(owner, way, piece, first):
        kind, start, size = piece
        rows = pl.ds(way * half + start, size)
        target = (packed_ref if kind == "p" else out_ref).at[owner, rows]
        if first:
            return (own_ref if kind == "p" else turned_ref).at[rows], target
        return target, target

    def hop(way, step, k):
        owner = at(place - step if way == 0 else place + step, core)
        source, target = views(owner, way, pieces[k], step == 0)
        return pltpu.make_async_remote_copy(
            src_ref=source,
            dst_ref=target,
            send_sem=send_sem.at[way, step, k],
            recv_sem=recv_sem.at[way, step, k],
            device_id=(right if way == 0 else left, side),
            device_id_type=MESH,
        )

    def across(way, step, k):
        owner = at(place - step if way == 0 else place + step, core)
        source, target = views(owner, way, pieces[k], step == 0)
        return pltpu.make_async_remote_copy(
            src_ref=source,
            dst_ref=target,
            send_sem=twin_send.at[way, step, k],
            recv_sem=twin_recv.at[way, step, k],
            device_id=(twin, side),
            device_id_type=MESH,
        )

    started = []
    for k in range(len(pieces)):
        for way in range(2):
            copy = hop(way, 0, k)
            copy.start()
            started.append(copy)
    rows_copy = pltpu.make_async_remote_copy(
        src_ref=normed_ref,
        dst_ref=whole_ref.at[side],
        send_sem=pair_sem.at[0],
        recv_sem=pair_sem.at[1],
        device_id=(me, partner),
        device_id_type=MESH,
    )
    rows_copy.start()
    locals_ = [
        pltpu.make_async_copy(own_ref, packed_ref.at[me], local_sem.at[0]),
        pltpu.make_async_copy(turned_ref, out_ref.at[me], local_sem.at[1]),
        pltpu.make_async_copy(normed_ref, whole_ref.at[side], local_sem.at[2]),
    ]
    for copy in locals_:
        copy.start()
    crossed = []
    for step in range(chips):
        for k in range(len(pieces)):
            for way in range(2):
                if step > 0:
                    hop(way, step - 1, k).wait_recv()
                    if step < chips - 1:
                        copy = hop(way, step, k)
                        copy.start()
                        started.append(copy)
                copy = across(way, step, k)
                copy.start()
                crossed.append(copy)
    for copy in locals_:
        copy.wait()
    for copy in started:
        copy.wait_send()
    for copy in crossed:
        copy.wait()
    rows_copy.wait()


def ring_gather(packed, turned, normed):
    count = lax.axis_size("req")
    chips = count // 2
    parts = packed.shape[0] // (2 * CHUNK) + 1
    anywhere = pl.BlockSpec(memory_space=pl.ANY)
    gathered, columns, whole = pl.pallas_call(
        lambda *refs: ring_kernel(count, *refs),
        out_shape=(
            jax.ShapeDtypeStruct((count,) + packed.shape, packed.dtype),
            jax.ShapeDtypeStruct((count,) + turned.shape, turned.dtype),
            jax.ShapeDtypeStruct((2,) + normed.shape, normed.dtype),
        ),
        in_specs=[anywhere] * 3,
        out_specs=(anywhere,) * 3,
        scratch_shapes=[
            pltpu.SemaphoreType.DMA((2, chips - 1, parts)),
            pltpu.SemaphoreType.DMA((2, chips - 1, parts)),
            pltpu.SemaphoreType.DMA((2, chips, parts)),
            pltpu.SemaphoreType.DMA((2, chips, parts)),
            pltpu.SemaphoreType.DMA((2,)),
            pltpu.SemaphoreType.DMA((3,)),
        ],
        compiler_params=pltpu.CompilerParams(collective_id=0, has_side_effects=True),
    )(packed, turned, normed)
    return (
        gathered.reshape(-1, packed.shape[1]),
        columns.reshape(-1, turned.shape[1]),
        whole.reshape(-1, normed.shape[1]),
    )


def gather_all(packed, out_proj, normed):
    if ring_fits(packed.shape[0]):
        spare = -packed.shape[1] % 128
        packed = jnp.pad(packed, ((0, 0), (0, spare)))
        return ring_gather(packed, out_proj.T, normed)
    return (
        lax.all_gather(packed, "req", axis=0, tiled=True),
        lax.all_gather(out_proj.T, "req", axis=0, tiled=True),
        lax.all_gather(normed, "mdl", axis=0, tiled=True),
    )


def swap(array):
    return lax.ppermute(array, "mdl", [(0, 1), (1, 0)])


def local(
    hidden,
    input_gain,
    gate_proj,
    value_proj,
    state_proj,
    step_proj,
    conv_value,
    conv_state,
    step_bias,
    decay_log,
    skip_gain,
    output_gain,
    out_proj,
    state_start,
    edge_value,
    edge_state,
    lengths,
    accepted,
):
    requests, heads_here, head_dim, nstate = state_start.shape
    rows_dev = hidden.shape[0]
    span = rows_dev * lax.axis_size("mdl") // requests
    here_count = rows_dev // span
    group_rows = requests * span
    inner_here = heads_here * head_dim
    width_k = conv_value.shape[0] - 1
    edge_count = width_k - 1
    my_index = lax.axis_index("mdl")
    floats = hidden.astype(jnp.float32)
    normed = (
        floats * lax.rsqrt(jnp.mean(floats * floats, -1, keepdims=True) + EPSILON) * input_gain
    ).astype(jnp.bfloat16)
    widths = (gate_proj.shape[1], value_proj.shape[1], state_proj.shape[1], step_proj.shape[1])
    first_end = widths[0]
    second_end = first_end + widths[1]
    third_end = second_end + widths[2]
    fourth_end = third_end + widths[3]
    packed = jnp.concatenate((gate_proj, value_proj, state_proj, step_proj), 1)
    joined_piece, out_turned, whole = gather_all(packed, out_proj, normed)
    joined = jnp.dot(whole, joined_piece, preferred_element_type=jnp.float32)
    gates = joined[:, :first_end].astype(jnp.bfloat16)
    values = joined[:, first_end:second_end].astype(jnp.bfloat16)
    readers = joined[:, second_end:third_end].astype(jnp.bfloat16)
    step_raw = joined[:, third_end:fourth_end].astype(jnp.bfloat16)
    current = jnp.concatenate([values, readers], 1).reshape(requests, span, -1)
    edges = jnp.concatenate([edge_value, edge_state], 2)
    extended = jnp.concatenate([edges, current], 1).astype(jnp.float32)
    taps = jnp.concatenate([conv_value, conv_state], 1)
    convolved = taps[width_k][None, None, :] + jnp.zeros(
        (requests, span, taps.shape[1]), jnp.float32
    )
    for shift in range(width_k):
        convolved = convolved + taps[shift][None, None, :] * extended[:, shift : shift + span]
    active = jax.nn.silu(convolved).astype(jnp.bfloat16)
    vals = active[..., :inner_here].reshape(requests, span, heads_here, head_dim)
    inputs_b = active[..., inner_here : inner_here + nstate]
    reads_c = active[..., inner_here + nstate :]
    vals_f = vals.astype(jnp.float32)
    steps = jax.nn.softplus(
        step_raw.astype(jnp.float32).reshape(requests, span, heads_here) + step_bias
    )
    logs = -steps * jnp.exp(decay_log)
    sooner = jnp.arange(span, dtype=jnp.int32)
    triangle = (sooner[:, None] >= sooner[None, :]).astype(jnp.float32)
    running = jnp.einsum("ts,gsh->gth", triangle, logs, precision=HIGHEST)
    intersection = jnp.einsum("gtn,gsn->gts", reads_c, inputs_b, preferred_element_type=jnp.float32)
    positions = jnp.arange(span, dtype=jnp.int32)
    lower = positions[:, None] >= positions[None, :]
    spread = jnp.where(
        lower[None, :, :, None], running[:, :, None, :] - running[:, None, :, :], -jnp.inf
    )
    kernel = intersection[..., None] * jnp.exp(spread) * steps[:, None, :, :]
    outputs = jnp.einsum(
        "gtsh,gshp->gthp", kernel.astype(jnp.bfloat16), vals, preferred_element_type=jnp.float32
    )
    carried = jnp.einsum(
        "gtn,ghpn->gthp",
        reads_c,
        state_start.astype(jnp.bfloat16),
        preferred_element_type=jnp.float32,
    )
    outputs = outputs + jnp.exp(running)[..., None] * carried + skip_gain[:, None] * vals_f
    product = outputs.reshape(group_rows, inner_here) * jax.nn.silu(gates.astype(jnp.float32))
    squares = jnp.sum(product * product, -1)
    gated = (product * output_gain).astype(jnp.bfloat16)
    paired = lax.axis_size("mdl") == 2
    total_squares = squares + swap(squares) if paired else lax.psum(squares, "mdl")
    scale = lax.rsqrt(total_squares / (inner_here * lax.axis_size("mdl")) + EPSILON)
    partial_terms = lax.dot_general(
        gated, out_turned, (((1,), (1,)), ((), ())), preferred_element_type=jnp.float32
    ).astype(jnp.bfloat16)
    if paired:
        theirs = lax.dynamic_slice_in_dim(
            partial_terms, (1 - my_index) * rows_dev, rows_dev, 0
        )
        mine = lax.dynamic_slice_in_dim(partial_terms, my_index * rows_dev, rows_dev, 0)
        mine = mine.astype(jnp.float32) + swap(theirs).astype(jnp.float32)
    else:
        mine = lax.psum_scatter(
            partial_terms, "mdl", scatter_dimension=0, tiled=True
        ).astype(jnp.float32)
    my_scale = lax.dynamic_slice_in_dim(scale, my_index * rows_dev, rows_dev, 0)
    my_lengths = lax.dynamic_slice_in_dim(lengths, my_index * here_count, here_count, 0)
    live = (positions[None, :] < my_lengths[:, None]).reshape(rows_dev).astype(jnp.float32)
    mixed = (mine * my_scale[:, None] * live[:, None]).astype(jnp.bfloat16)
    last = accepted - 1
    chosen = (positions[None, :] == last[:, None]).astype(jnp.float32)
    running_last = jnp.sum(chosen[:, :, None] * running, axis=1)
    before = positions[None, :] <= last[:, None]
    reach = jnp.where(before[:, :, None], running_last[:, None, :] - running, -jnp.inf)
    weights_s = jnp.exp(reach) * steps
    gathered_state = jnp.einsum(
        "gshp,gsn->ghpn",
        (weights_s[..., None] * vals_f).astype(jnp.bfloat16),
        inputs_b,
        preferred_element_type=jnp.float32,
    )
    state_here = jnp.exp(running_last)[:, :, None, None] * state_start + gathered_state
    picks = accepted[:, None] + jnp.arange(edge_count, dtype=jnp.int32)[None, :]
    selected = jnp.take_along_axis(extended, picks[:, :, None], axis=1)
    if paired:
        def to_owner(array, kind):
            sent = lax.dynamic_slice_in_dim(array, (1 - my_index) * here_count, here_count, 0)
            kept = lax.dynamic_slice_in_dim(array, my_index * here_count, here_count, 0)
            come = swap(sent.astype(jnp.bfloat16)).astype(kind)
            kept = kept.astype(kind)
            first = my_index == 0
            return jnp.where(first, kept, come), jnp.where(first, come, kept)

        state_final = jnp.concatenate(to_owner(state_here, jnp.float32), 1)
        edges_home = jnp.concatenate(to_owner(selected[..., :inner_here], selected.dtype), 2)
    else:
        value_edges = selected[..., :inner_here].reshape(requests, edge_count, heads_here, head_dim)
        value_edges = value_edges.transpose(0, 2, 1, 3).reshape(
            requests, heads_here, edge_count * head_dim
        )
        states_home, edges_home = (
            lax.all_to_all(
                state_here.reshape(requests, heads_here, head_dim * nstate).astype(jnp.bfloat16),
                "mdl",
                split_axis=0,
                concat_axis=1,
                tiled=True,
            ).astype(jnp.float32),
            lax.all_to_all(
                value_edges.astype(jnp.bfloat16), "mdl", split_axis=0, concat_axis=1, tiled=True
            ).astype(value_edges.dtype),
        )
        heads_all = states_home.shape[1]
        state_final = states_home.reshape(here_count, heads_all, head_dim, nstate)
        edges_home = edges_home.reshape(here_count, heads_all, edge_count, head_dim).transpose(
            0, 2, 1, 3
        )
        edges_home = edges_home.reshape(here_count, edge_count, heads_all * head_dim)
    state_edges = lax.dynamic_slice_in_dim(
        selected[..., inner_here:], my_index * here_count, here_count, 0
    )
    edge_final = jnp.concatenate([edges_home, state_edges], 2).astype(jnp.bfloat16)
    return (mixed, state_final, edge_final)


def solution(mesh):
    return jax.shard_map(
        local,
        mesh=mesh,
        in_specs=(
            P(("req", "mdl"), None),
            P(),
            P("req", "mdl"),
            P("req", "mdl"),
            P("req", None),
            P("req", "mdl"),
            P(None, "mdl"),
            P(),
            P("mdl"),
            P("mdl"),
            P("mdl"),
            P("mdl"),
            P("mdl", "req"),
            P("req", "mdl", None, None),
            P("req", None, "mdl"),
            P("req", None, None),
            P("req"),
            P("req"),
        ),
        out_specs=(
            P(("req", "mdl"), None),
            P(("req", "mdl"), None, None, None),
            P(("req", "mdl"), None, None),
        ),
        check_vma=False,
    )
```

```python
import jax
import jax.numpy as jnp
from jax import lax
from jax.experimental import pallas as pl
from jax.experimental.pallas import tpu as pltpu
from jax.sharding import PartitionSpec as P

EPSILON = 1e-05
HIGHEST = lax.Precision.HIGHEST
MESH = pl.DeviceIdType.MESH
CHUNK = 16


def ring_fits(rows):
    return (
        lax.axis_size("mdl") == 2
        and lax.axis_size("req") % 4 == 0
        and lax.axis_size("req") >= 8
        and rows % (2 * CHUNK) == 0
    )


def ring_kernel(
    count,
    own_ref,
    turned_ref,
    normed_ref,
    packed_ref,
    out_ref,
    whole_ref,
    send_sem,
    recv_sem,
    twin_send,
    twin_recv,
    pair_sem,
    local_sem,
):
    chips = count // 2
    depth = chips // 2
    me = lax.axis_index("req")
    side = lax.axis_index("mdl")
    core = me % 2
    chip = me // 2
    x = chip % 2
    z = chip // 2
    place = z + x * (chips - 1 - 2 * z)

    def at(spot, which):
        spot = (spot + 2 * chips) % chips
        far = spot // depth
        level = spot + far * (chips - 1 - 2 * spot)
        return (level * 2 + far) * 2 + which

    right, left, twin = at(place + 1, core), at(place - 1, core), at(place, 1 - core)
    partner = 1 - side
    barrier = pltpu.get_barrier_semaphore()
    for other in (right, left, twin):
        pl.semaphore_signal(barrier, inc=1, device_id=(other, side), device_id_type=MESH)
    pl.semaphore_signal(barrier, inc=1, device_id=(me, partner), device_id_type=MESH)
    pl.semaphore_wait(barrier, 4)

    half = own_ref.shape[0] // 2
    pieces = [("p", k * CHUNK, CHUNK) for k in range(half // CHUNK)] + [("o", 0, half)]

    def views(owner, way, piece, first):
        kind, start, size = piece
        rows = pl.ds(way * half + start, size)
        target = (packed_ref if kind == "p" else out_ref).at[owner, rows]
        if first:
            return (own_ref if kind == "p" else turned_ref).at[rows], target
        return target, target

    def hop(way, step, k):
        owner = at(place - step if way == 0 else place + step, core)
        source, target = views(owner, way, pieces[k], step == 0)
        return pltpu.make_async_remote_copy(
            src_ref=source,
            dst_ref=target,
            send_sem=send_sem.at[way, step, k],
            recv_sem=recv_sem.at[way, step, k],
            device_id=(right if way == 0 else left, side),
            device_id_type=MESH,
        )

    def across(way, step, k):
        owner = at(place - step if way == 0 else place + step, core)
        source, target = views(owner, way, pieces[k], step == 0)
        return pltpu.make_async_remote_copy(
            src_ref=source,
            dst_ref=target,
            send_sem=twin_send.at[way, step, k],
            recv_sem=twin_recv.at[way, step, k],
            device_id=(twin, side),
            device_id_type=MESH,
        )

    started = []
    for k in range(len(pieces)):
        for way in range(2):
            copy = hop(way, 0, k)
            copy.start()
            started.append(copy)
    rows_copy = pltpu.make_async_remote_copy(
        src_ref=normed_ref,
        dst_ref=whole_ref.at[side],
        send_sem=pair_sem.at[0],
        recv_sem=pair_sem.at[1],
        device_id=(me, partner),
        device_id_type=MESH,
    )
    rows_copy.start()
    locals_ = [
        pltpu.make_async_copy(own_ref, packed_ref.at[me], local_sem.at[0]),
        pltpu.make_async_copy(turned_ref, out_ref.at[me], local_sem.at[1]),
        pltpu.make_async_copy(normed_ref, whole_ref.at[side], local_sem.at[2]),
    ]
    for copy in locals_:
        copy.start()
    crossed = []
    for step in range(chips):
        for k in range(len(pieces)):
            for way in range(2):
                if step > 0:
                    hop(way, step - 1, k).wait_recv()
                    if step < chips - 1:
                        copy = hop(way, step, k)
                        copy.start()
                        started.append(copy)
                copy = across(way, step, k)
                copy.start()
                crossed.append(copy)
    for copy in locals_:
        copy.wait()
    for copy in started:
        copy.wait_send()
    for copy in crossed:
        copy.wait()
    rows_copy.wait()


def ring_gather(packed, turned, normed):
    count = lax.axis_size("req")
    chips = count // 2
    parts = packed.shape[0] // (2 * CHUNK) + 1
    anywhere = pl.BlockSpec(memory_space=pl.ANY)
    gathered, columns, whole = pl.pallas_call(
        lambda *refs: ring_kernel(count, *refs),
        out_shape=(
            jax.ShapeDtypeStruct((count,) + packed.shape, packed.dtype),
            jax.ShapeDtypeStruct((count,) + turned.shape, turned.dtype),
            jax.ShapeDtypeStruct((2,) + normed.shape, normed.dtype),
        ),
        in_specs=[anywhere] * 3,
        out_specs=(anywhere,) * 3,
        scratch_shapes=[
            pltpu.SemaphoreType.DMA((2, chips - 1, parts)),
            pltpu.SemaphoreType.DMA((2, chips - 1, parts)),
            pltpu.SemaphoreType.DMA((2, chips, parts)),
            pltpu.SemaphoreType.DMA((2, chips, parts)),
            pltpu.SemaphoreType.DMA((2,)),
            pltpu.SemaphoreType.DMA((3,)),
        ],
        compiler_params=pltpu.CompilerParams(collective_id=0, has_side_effects=True),
    )(packed, turned, normed)
    return (
        gathered.reshape(-1, packed.shape[1]),
        columns.reshape(-1, turned.shape[1]),
        whole.reshape(-1, normed.shape[1]),
    )


def gather_all(packed, out_proj, normed):
    if ring_fits(packed.shape[0]):
        spare = -packed.shape[1] % 128
        packed = jnp.pad(packed, ((0, 0), (0, spare)))
        return ring_gather(packed, out_proj.T, normed)
    return (
        lax.all_gather(packed, "req", axis=0, tiled=True),
        lax.all_gather(out_proj.T, "req", axis=0, tiled=True),
        lax.all_gather(normed, "mdl", axis=0, tiled=True),
    )


def swap(array):
    return lax.ppermute(array, "mdl", [(0, 1), (1, 0)])


def local(
    hidden,
    input_gain,
    gate_proj,
    value_proj,
    state_proj,
    step_proj,
    conv_value,
    conv_state,
    step_bias,
    decay_log,
    skip_gain,
    output_gain,
    out_proj,
    state_start,
    edge_value,
    edge_state,
    lengths,
    accepted,
):
    requests, heads_here, head_dim, nstate = state_start.shape
    rows_dev = hidden.shape[0]
    span = rows_dev * lax.axis_size("mdl") // requests
    here_count = rows_dev // span
    group_rows = requests * span
    inner_here = heads_here * head_dim
    width_k = conv_value.shape[0] - 1
    edge_count = width_k - 1
    my_index = lax.axis_index("mdl")
    floats = hidden.astype(jnp.float32)
    normed = (
        floats * lax.rsqrt(jnp.mean(floats * floats, -1, keepdims=True) + EPSILON) * input_gain
    ).astype(jnp.bfloat16)
    widths = (gate_proj.shape[1], value_proj.shape[1], state_proj.shape[1], step_proj.shape[1])
    first_end = widths[0]
    second_end = first_end + widths[1]
    third_end = second_end + widths[2]
    fourth_end = third_end + widths[3]
    packed = jnp.concatenate((gate_proj, value_proj, state_proj, step_proj), 1)
    joined_piece, out_turned, whole = gather_all(packed, out_proj, normed)
    joined = jnp.dot(whole, joined_piece, preferred_element_type=jnp.float32)
    gates = joined[:, :first_end].astype(jnp.bfloat16)
    values = joined[:, first_end:second_end].astype(jnp.bfloat16)
    readers = joined[:, second_end:third_end].astype(jnp.bfloat16)
    step_raw = joined[:, third_end:fourth_end].astype(jnp.bfloat16)
    current = jnp.concatenate([values, readers], 1).reshape(requests, span, -1)
    edges = jnp.concatenate([edge_value, edge_state], 2)
    extended = jnp.concatenate([edges, current], 1).astype(jnp.float32)
    taps = jnp.concatenate([conv_value, conv_state], 1)
    convolved = taps[width_k][None, None, :] + jnp.zeros(
        (requests, span, taps.shape[1]), jnp.float32
    )
    for shift in range(width_k):
        convolved = convolved + taps[shift][None, None, :] * extended[:, shift : shift + span]
    active = jax.nn.silu(convolved).astype(jnp.bfloat16)
    vals = active[..., :inner_here].reshape(requests, span, heads_here, head_dim)
    inputs_b = active[..., inner_here : inner_here + nstate]
    reads_c = active[..., inner_here + nstate :]
    vals_f = vals.astype(jnp.float32)
    steps = jax.nn.softplus(
        step_raw.astype(jnp.float32).reshape(requests, span, heads_here) + step_bias
    )
    logs = -steps * jnp.exp(decay_log)
    sooner = jnp.arange(span, dtype=jnp.int32)
    triangle = (sooner[:, None] >= sooner[None, :]).astype(jnp.float32)
    running = jnp.einsum("ts,gsh->gth", triangle, logs, precision=HIGHEST)
    intersection = jnp.einsum("gtn,gsn->gts", reads_c, inputs_b, preferred_element_type=jnp.float32)
    positions = jnp.arange(span, dtype=jnp.int32)
    lower = positions[:, None] >= positions[None, :]
    spread = jnp.where(
        lower[None, :, :, None], running[:, :, None, :] - running[:, None, :, :], -jnp.inf
    )
    kernel = intersection[..., None] * jnp.exp(spread) * steps[:, None, :, :]
    outputs = jnp.einsum(
        "gtsh,gshp->gthp", kernel.astype(jnp.bfloat16), vals, preferred_element_type=jnp.float32
    )
    carried = jnp.einsum(
        "gtn,ghpn->gthp",
        reads_c,
        state_start.astype(jnp.bfloat16),
        preferred_element_type=jnp.float32,
    )
    outputs = outputs + jnp.exp(running)[..., None] * carried + skip_gain[:, None] * vals_f
    product = outputs * jax.nn.silu(gates.astype(jnp.float32).reshape(outputs.shape))
    squares = jnp.sum(product * product, (2, 3)).reshape(group_rows)
    gated = (product * output_gain.reshape(heads_here, head_dim)).astype(jnp.bfloat16)
    gated = gated.reshape(group_rows, inner_here)
    paired = lax.axis_size("mdl") == 2
    total_squares = squares + swap(squares) if paired else lax.psum(squares, "mdl")
    scale = lax.rsqrt(total_squares / (inner_here * lax.axis_size("mdl")) + EPSILON)
    partial_terms = lax.dot_general(
        gated, out_turned, (((1,), (1,)), ((), ())), preferred_element_type=jnp.float32
    ).astype(jnp.bfloat16)
    if paired:
        theirs = lax.dynamic_slice_in_dim(
            partial_terms, (1 - my_index) * rows_dev, rows_dev, 0
        )
        mine = lax.dynamic_slice_in_dim(partial_terms, my_index * rows_dev, rows_dev, 0)
        mine = mine.astype(jnp.float32) + swap(theirs).astype(jnp.float32)
    else:
        mine = lax.psum_scatter(
            partial_terms, "mdl", scatter_dimension=0, tiled=True
        ).astype(jnp.float32)
    my_scale = lax.dynamic_slice_in_dim(scale, my_index * rows_dev, rows_dev, 0)
    my_lengths = lax.dynamic_slice_in_dim(lengths, my_index * here_count, here_count, 0)
    live = (positions[None, :] < my_lengths[:, None]).reshape(rows_dev).astype(jnp.float32)
    mixed = (mine * my_scale[:, None] * live[:, None]).astype(jnp.bfloat16)
    last = accepted - 1
    chosen = (positions[None, :] == last[:, None]).astype(jnp.float32)
    running_last = jnp.sum(chosen[:, :, None] * running, axis=1)
    before = positions[None, :] <= last[:, None]
    reach = jnp.where(before[:, :, None], running_last[:, None, :] - running, -jnp.inf)
    weights_s = jnp.exp(reach) * steps
    gathered_state = jnp.einsum(
        "gshp,gsn->ghpn",
        (weights_s[..., None] * vals_f).astype(jnp.bfloat16),
        inputs_b,
        preferred_element_type=jnp.float32,
    )
    state_here = jnp.exp(running_last)[:, :, None, None] * state_start + gathered_state
    picks = accepted[:, None] + jnp.arange(edge_count, dtype=jnp.int32)[None, :]
    selected = jnp.take_along_axis(extended, picks[:, :, None], axis=1)
    if paired:
        def to_owner(array, kind):
            sent = lax.dynamic_slice_in_dim(array, (1 - my_index) * here_count, here_count, 0)
            kept = lax.dynamic_slice_in_dim(array, my_index * here_count, here_count, 0)
            come = swap(sent.astype(jnp.bfloat16)).astype(kind)
            kept = kept.astype(kind)
            first = my_index == 0
            return jnp.where(first, kept, come), jnp.where(first, come, kept)

        state_final = jnp.concatenate(to_owner(state_here, jnp.float32), 1)
        edges_home = jnp.concatenate(to_owner(selected[..., :inner_here], selected.dtype), 2)
    else:
        value_edges = selected[..., :inner_here].reshape(requests, edge_count, heads_here, head_dim)
        value_edges = value_edges.transpose(0, 2, 1, 3).reshape(
            requests, heads_here, edge_count * head_dim
        )
        states_home, edges_home = (
            lax.all_to_all(
                state_here.reshape(requests, heads_here, head_dim * nstate).astype(jnp.bfloat16),
                "mdl",
                split_axis=0,
                concat_axis=1,
                tiled=True,
            ).astype(jnp.float32),
            lax.all_to_all(
                value_edges.astype(jnp.bfloat16), "mdl", split_axis=0, concat_axis=1, tiled=True
            ).astype(value_edges.dtype),
        )
        heads_all = states_home.shape[1]
        state_final = states_home.reshape(here_count, heads_all, head_dim, nstate)
        edges_home = edges_home.reshape(here_count, heads_all, edge_count, head_dim).transpose(
            0, 2, 1, 3
        )
        edges_home = edges_home.reshape(here_count, edge_count, heads_all * head_dim)
    state_edges = lax.dynamic_slice_in_dim(
        selected[..., inner_here:], my_index * here_count, here_count, 0
    )
    edge_final = jnp.concatenate([edges_home, state_edges], 2).astype(jnp.bfloat16)
    return (mixed, state_final, edge_final)


def solution(mesh):
    return jax.shard_map(
        local,
        mesh=mesh,
        in_specs=(
            P(("req", "mdl"), None),
            P(),
            P("req", "mdl"),
            P("req", "mdl"),
            P("req", None),
            P("req", "mdl"),
            P(None, "mdl"),
            P(),
            P("mdl"),
            P("mdl"),
            P("mdl"),
            P("mdl"),
            P("mdl", "req"),
            P("req", "mdl", None, None),
            P("req", None, "mdl"),
            P("req", None, None),
            P("req"),
            P("req"),
        ),
        out_specs=(
            P(("req", "mdl"), None),
            P(("req", "mdl"), None, None, None),
            P(("req", "mdl"), None, None),
        ),
        check_vma=False,
    )
```
